32 devices in a mesh: row: 4 (over y, x), col: 8 (over z, core).
Axes of the slice: x: 2, y: 2, z: 4, core: 2. Of those that a mesh axis runs over, the one named last changes fastest.
Arguments:
- hidden_states: bfloat16 [512, 5120], P('row', 'col'), may hold values from -6 to 6
- clip_lengths: int32 [4, 2], P('row'), may hold values from 1 to 64, as said below
- modulation: bfloat16 [8, 3, 5120], P('row', None, 'col'), may hold values from -4 to 4
- fc1_weight: bfloat16 [5120, 13824], P('row', 'col'), may hold values from -0.078125 to 0.078125
- fc2_weight: bfloat16 [13824, 5120], P('col', 'row'), may hold values from -0.0546875 to 0.0546875
- out_grad: bfloat16 [512, 5120], P('row', 'col'), may hold values from -6 to 6
Outputs:
- block_out: bfloat16 [512, 5120], P('row', 'col')
- input_grad: bfloat16 [512, 5120], P('row', 'col')
- modulation_grad: float32 [8, 3, 5120], P('row', None, 'col')
The draws below stay inside these ranges and needn't reach their ends.
Inputs may be any that keep to these rules, and one draw needn't show every extreme that they name: `clip_lengths`: in every draw the clip windows of some grid row all have 64 tokens.
All inputs are finite; a program needn't handle non-finite values.
Results may differ from the reference program's by a relative error of at most 0.0055.
Values may be sent and summed in bfloat16 or wider, within the bound.
No kernel may reach another device: no remote copies, remote signals or barrier semaphores. Data moves between devices by JAX's collectives and lax.ppermute only.
A program may use at most 128 MiB of HBM per device.

```python
import jax
import jax.numpy as jnp
from jax import lax

D = 5120
FF = 13824
TOK_ROW = 128
CLIPS_ROW = 2
MOST = 64
GRID_ROWS = 4
TOKENS = 512
CLIPS = 8


def draw_clip_lengths(key, part):
    counts = jax.random.randint(key, (GRID_ROWS, CLIPS_ROW), 1, MOST + 1)
    full_row = jax.random.randint(jax.random.fold_in(key, 7), (), 0, GRID_ROWS)
    chosen = jnp.arange(GRID_ROWS, dtype=jnp.int32)[:, None] == full_row
    return jnp.where(chosen, MOST, counts).astype(jnp.int32)


def shard_levels(stream_key, dims, cuts, least, high):
    factor_of = 1.0
    for position, blocks in cuts:
        draws = jax.random.uniform(jax.random.fold_in(jax.random.fold_in(stream_key, 6), position), (blocks,), jnp.float32, least / len(cuts), high / len(cuts))
        factor_of = factor_of * jnp.repeat(jnp.exp(draws), dims[position] // blocks).reshape((-1,) + (1,) * (len(dims) - 1 - position))
    return factor_of


def scatter_about(own_key, shape, scale, most, cuts=(), kind=jnp.bfloat16):
    entries = jax.random.normal(own_key, shape, jnp.float32) * scale
    if len(cuts) > 0:
        entries = shard_levels(own_key, shape, cuts, -0.22, 0.18) * entries
    return jnp.clip(entries, min=-most, max=most).astype(kind)


def setup_inputs(seed: int = 0) -> dict:
    splits = jax.random.split(jax.random.key(seed), 7)
    hidden_states = scatter_about(splits[0], (TOKENS, D), 1.0, 6.0, ((0, 4), (1, 8)))
    clip_lengths = draw_clip_lengths(jax.random.fold_in(splits[6], 71), 0)
    modulation = scatter_about(splits[2], (CLIPS, 3, D), 0.8, 4.0, ((0, 4), (2, 8)))
    fc1_weight = scatter_about(splits[3], (D, FF), D ** -0.5, 0.078125, ((0, 4), (1, 8)))
    fc2_weight = scatter_about(splits[4], (FF, D), FF ** -0.5, 0.0546875, ((0, 8), (1, 4)))
    out_grad = scatter_about(splits[5], (TOKENS, D), 1.0, 6.0, ((0, 4), (1, 8)))
    return dict(hidden_states=hidden_states, clip_lengths=clip_lengths, modulation=modulation, fc1_weight=fc1_weight, fc2_weight=fc2_weight, out_grad=out_grad)


epsilon = 1e-06

def gelu_slope(value):
    coeff = 0.7978845608028654
    inner = coeff * (value + 0.044715 * value * value * value)
    tangent = jnp.tanh(inner)
    return 0.5 * (1.0 + tangent) + 0.5 * value * (1.0 - tangent * tangent) * coeff * (1.0 + 3.0 * 0.044715 * value * value)

def reference(hidden_states, clip_lengths, modulation, fc1_weight, fc2_weight, out_grad):
    clip_ends = jnp.cumsum(clip_lengths, axis=1).astype(jnp.int32)
    places = jnp.arange(TOK_ROW, dtype=jnp.int32)
    segment = lax.optimization_barrier(jnp.sum((places[None, :, None] >= clip_ends[:, None, :]).astype(jnp.int32), axis=2))
    onehot = (segment[:, :, None] == jnp.arange(CLIPS_ROW, dtype=jnp.int32)[None, None, :]).astype(jnp.float32)
    live_rows = (segment < CLIPS_ROW).astype(jnp.float32).reshape(TOKENS, 1)
    mod_rows = modulation.astype(jnp.float32).reshape(GRID_ROWS, CLIPS_ROW, 3 * D)
    token_mod = jnp.einsum('gtc,gcd->gtd', onehot, mod_rows).reshape(TOKENS, 3, D)
    shift_tok = token_mod[:, 0]
    scale_tok = token_mod[:, 1]
    gate_tok = token_mod[:, 2]
    x_float = hidden_states.astype(jnp.float32)
    centre = lax.optimization_barrier(jnp.mean(x_float, axis=1, keepdims=True))
    deviation = x_float - centre
    inverse = lax.rsqrt(lax.optimization_barrier(jnp.mean(deviation * deviation, axis=1, keepdims=True)) + epsilon)
    normed = deviation * inverse
    modulated = (normed * (1.0 + scale_tok) + shift_tok).astype(jnp.bfloat16)
    pre_act = jnp.dot(modulated, fc1_weight, preferred_element_type=jnp.float32)
    activated = jax.nn.gelu(pre_act, approximate=True).astype(jnp.bfloat16)
    projected = jnp.dot(activated, fc2_weight, preferred_element_type=jnp.float32)
    block_out = (live_rows * (x_float + gate_tok * projected)).astype(jnp.bfloat16)
    grad_float = out_grad.astype(jnp.float32)
    z_grad = (live_rows * gate_tok * grad_float).astype(jnp.bfloat16)
    act_grad = lax.dot_general(z_grad, fc2_weight, (((1,), (1,)), ((), ())), preferred_element_type=jnp.float32)
    pre_grad = (act_grad * gelu_slope(pre_act)).astype(jnp.bfloat16)
    mod_in_grad = lax.dot_general(pre_grad, fc1_weight, (((1,), (1,)), ((), ())), preferred_element_type=jnp.float32)
    norm_grad = mod_in_grad * (1.0 + scale_tok)
    first_mean = lax.optimization_barrier(jnp.mean(norm_grad, axis=1, keepdims=True))
    second_mean = lax.optimization_barrier(jnp.mean(norm_grad * normed, axis=1, keepdims=True))
    input_grad = (live_rows * (grad_float + inverse * (norm_grad - first_mean - normed * second_mean))).astype(jnp.bfloat16)
    shift_grad = jnp.einsum('gtc,gtd->gcd', onehot, mod_in_grad.reshape(GRID_ROWS, TOK_ROW, D))
    scale_grad = jnp.einsum('gtc,gtd->gcd', onehot, (mod_in_grad * normed).reshape(GRID_ROWS, TOK_ROW, D))
    gate_grad = jnp.einsum('gtc,gtd->gcd', onehot, (projected * grad_float).reshape(GRID_ROWS, TOK_ROW, D))
    modulation_grad = jnp.stack([shift_grad, scale_grad, gate_grad], axis=2).reshape(CLIPS, 3, D)
    return (block_out, input_grad, modulation_grad)
```

```python
import jax
import jax.numpy as jnp
from jax import lax
from jax.sharding import PartitionSpec as P

epsilon = 1e-06
BF = jnp.bfloat16
F32 = jnp.float32


def gelu_and_slope(value):
    coeff = 0.7978845608028654
    inner = coeff * (value + 0.044715 * value * value * value)
    tangent = jnp.tanh(inner)
    half = 0.5 * (1.0 + tangent)
    slope = half + 0.5 * value * (1.0 - tangent * tangent) * coeff * (
        1.0 + 3.0 * 0.044715 * value * value
    )
    return value * half, slope


def make_body(rows, cols):
    depth = cols // 2
    bits = [1 << b for b in range(rows.bit_length() - 1)]

    def over_row(value, flip):
        return lax.ppermute(value, "row", [(i, i ^ flip) for i in range(rows)])

    def over_z(value, flip):
        return lax.ppermute(value, "col", [(i, i ^ (2 * flip)) for i in range(cols)])

    def over_core(value):
        return lax.ppermute(value, "col", [(i, i ^ 1) for i in range(cols)])

    def transpose_owner(value):
        pairs = []
        for r in range(rows):
            for c in range(cols):
                pairs.append((r * cols + c, (c // 2) * cols + 2 * r + c % 2))
        return lax.ppermute(value, ("row", "col"), pairs)

    def reduce_rows(blocks, order):
        blocks = dict(enumerate(blocks))
        for flip in order:
            sent = [j for j in sorted(blocks) if j & flip]
            came = over_row(jnp.stack([blocks[j].astype(BF) for j in sent]), flip)
            for place, j in enumerate(sent):
                blocks[j ^ flip] = blocks[j ^ flip] + came[place].astype(F32)
                del blocks[j]
        return blocks[0]

    def gather_rows(value, order):
        have = {0: value}
        for flip in order:
            sent = sorted(have)
            came = over_row(jnp.stack([have[j] for j in sent]), flip)
            for place, j in enumerate(sent):
                have[j ^ flip] = came[place]
        return [have[j] for j in range(rows)]

    def reduce_scatter_rows(share, tok_rows):
        half = tok_rows // 2
        parts = share.reshape(rows, tok_rows, share.shape[1])
        first = reduce_rows([parts[j, :half] for j in range(rows)], bits)
        second = reduce_rows([parts[j, half:] for j in range(rows)], bits[::-1])
        return jnp.concatenate([first, second], axis=0)

    def all_gather_rows(value):
        half = value.shape[0] // 2
        first = gather_rows(value[:half], bits)
        second = gather_rows(value[half:], bits[::-1])
        return jnp.concatenate([p for pair in zip(first, second) for p in pair], axis=0)

    def body(hidden_states, clip_lengths, modulation, fc1_weight, fc2_weight, out_grad):
        tok_rows, width = hidden_states.shape
        clip_count = modulation.shape[0]
        full_width = width * cols
        r = lax.axis_index("row")
        c = lax.axis_index("col")
        z, core = c // 2, c % 2

        clip_ends = jnp.cumsum(clip_lengths[0])
        places = jnp.arange(tok_rows, dtype=jnp.int32)
        segment = jnp.sum((places[:, None] >= clip_ends[None, :]).astype(jnp.int32), axis=1)
        onehot = (segment[:, None] == jnp.arange(clip_count, dtype=jnp.int32)[None, :]).astype(F32)
        live = (segment < clip_count).astype(F32)[:, None]

        def per_token(vectors):
            total = onehot[:, 0:1] * vectors[0:1].astype(F32)
            for i in range(1, clip_count):
                total = total + onehot[:, i : i + 1] * vectors[i : i + 1].astype(F32)
            return total

        def to_rows(pick):
            got = [pick(r)] + [over_row(pick(r ^ i), i) for i in range(1, rows)]
            own = jnp.concatenate(got, axis=0)
            other = over_core(own)
            low = jnp.where(core == 0, own, other)
            high = jnp.where(core == 0, other, own)
            return jnp.concatenate([low, high], axis=1)

        def to_owner(share):
            low, high = share[:, :width], share[:, width:]
            kept = jnp.where(core == 0, low, high)
            given = jnp.where(core == 0, high, low)
            both = kept + over_core(given.astype(BF)).astype(F32)
            both = both.reshape(rows, tok_rows, width)

            def group(flip):
                return lax.dynamic_index_in_dim(both, r ^ z ^ flip, 0, keepdims=False)

            total = group(0)
            for flip in range(1, depth):
                total = total + over_z(group(flip).astype(BF), flip).astype(F32)
            return transpose_owner(total.astype(BF)).astype(F32)

        x_here = hidden_states.astype(F32)
        g_here = out_grad.astype(F32)
        scale_here = per_token(modulation[:, 1])
        gate_here = per_token(modulation[:, 2])

        fill = -(tok_rows + 2 * clip_count) % 16
        packed = jnp.concatenate(
            [hidden_states, modulation[:, 0], modulation[:, 1], jnp.zeros((fill, width), BF)], axis=0
        )
        chunks = jnp.stack([packed] + [over_z(packed, i) for i in range(1, depth)])
        x_part = chunks[:, :tok_rows].astype(F32)
        mean_part = jnp.mean(x_part, axis=(0, 2))
        spread = x_part - mean_part[None, :, None]
        square_part = jnp.sum(spread * spread, axis=(0, 2))
        theirs = over_core(jnp.stack([mean_part, square_part]))
        centre = 0.5 * (mean_part + theirs[0])
        gap = mean_part - theirs[0]
        square = square_part + theirs[1] + gap * gap * (full_width / 4)
        inverse = lax.rsqrt(square / full_width + epsilon)[:, None]
        centre = centre[:, None]
        normed = (x_here - centre) * inverse

        def pick_modulated(j):
            chunk = lax.dynamic_index_in_dim(chunks, z ^ j, 0, keepdims=False)
            shift = per_token(chunk[tok_rows : tok_rows + clip_count])
            scale = per_token(chunk[tok_rows + clip_count : tok_rows + 2 * clip_count])
            x = chunk[:tok_rows].astype(F32)
            return ((x - centre) * inverse * (1.0 + scale) + shift).astype(BF)

        z_grad = (live * gate_here * g_here).astype(BF)
        z_grad, _ = lax.optimization_barrier((z_grad, chunks))
        z_chunks = jnp.stack([z_grad] + [over_z(z_grad, i) for i in range(1, depth)])

        def pick_z_grad(j):
            return lax.dynamic_index_in_dim(z_chunks, z ^ j, 0, keepdims=False)

        modulated = to_rows(pick_modulated)
        pre_share = jnp.dot(modulated, fc1_weight, preferred_element_type=F32)
        pre_act = reduce_scatter_rows(pre_share, tok_rows)
        z_rows = to_rows(pick_z_grad)
        act_share = lax.dot_general(
            z_rows, fc2_weight, (((1,), (1,)), ((), ())), preferred_element_type=F32
        )
        act_grad = reduce_scatter_rows(act_share, tok_rows)
        activated, slope = gelu_and_slope(pre_act)
        activated_rows = all_gather_rows(activated.astype(BF))
        pre_grad_rows = all_gather_rows((act_grad * slope).astype(BF))
        in_share = lax.dot_general(
            pre_grad_rows, fc1_weight, (((1,), (1,)), ((), ())), preferred_element_type=F32
        )
        out_share = jnp.dot(activated_rows, fc2_weight, preferred_element_type=F32)
        mod_in_grad = to_owner(in_share)
        projected = to_owner(out_share)

        block_out = (live * (x_here + gate_here * projected)).astype(BF)
        norm_grad = mod_in_grad * (1.0 + scale_here)
        sums = jnp.stack([jnp.sum(norm_grad, axis=1), jnp.sum(norm_grad * normed, axis=1)])
        sums = sums + over_core(sums)
        sums = sums + sum(over_z(sums, i) for i in range(1, depth))
        first_mean = (sums[0] / full_width)[:, None]
        second_mean = (sums[1] / full_width)[:, None]
        input_grad = (
            live * (g_here + inverse * (norm_grad - first_mean - normed * second_mean))
        ).astype(BF)

        def per_clip(values):
            return jnp.stack(
                [jnp.sum(onehot[:, i : i + 1] * values, axis=0) for i in range(clip_count)]
            )

        modulation_grad = jnp.stack(
            [per_clip(mod_in_grad), per_clip(mod_in_grad * normed), per_clip(projected * g_here)],
            axis=1,
        )
        return (block_out, input_grad, modulation_grad)

    return body


def solution(mesh):
    rows, cols = mesh.shape["row"], mesh.shape["col"]
    return jax.shard_map(
        make_body(rows, cols),
        mesh=mesh,
        in_specs=(
            P("row", "col"),
            P("row", None),
            P("row", None, "col"),
            P("row", "col"),
            P("col", "row"),
            P("row", "col"),
        ),
        out_specs=(P("row", "col"), P("row", "col"), P("row", None, "col")),
        check_vma=False,
    )
```

```python
import jax
import jax.numpy as jnp
from jax import lax
from jax.sharding import PartitionSpec as P

epsilon = 1e-06
BF = jnp.bfloat16
F32 = jnp.float32


def gelu_and_slope(value):
    coeff = 0.7978845608028654
    inner = coeff * (value + 0.044715 * value * value * value)
    tangent = jnp.tanh(inner)
    half = 0.5 * (1.0 + tangent)
    slope = half + 0.5 * value * (1.0 - tangent * tangent) * coeff * (
        1.0 + 3.0 * 0.044715 * value * value
    )
    return value * half, slope


def dot(a, b):
    return jnp.dot(a, b, preferred_element_type=F32)


def dot_t(a, b):
    return lax.dot_general(a, b, (((1,), (1,)), ((), ())), preferred_element_type=F32)


def make_body(rows, cols):
    depth = cols // 2
    assert depth == rows and rows & (rows - 1) == 0

    def over_row(value, flip):
        return lax.ppermute(value, "row", [(i, i ^ flip) for i in range(rows)])

    def over_z(value, flip):
        return lax.ppermute(value, "col", [(i, i ^ (2 * flip)) for i in range(cols)])

    def over_core(value):
        return lax.ppermute(value, "col", [(i, i ^ 1) for i in range(cols)])

    def transpose_owner(value):
        pairs = []
        for r in range(rows):
            for c in range(cols):
                pairs.append((r * cols + c, (c // 2) * cols + 2 * r + c % 2))
        return lax.ppermute(value, ("row", "col"), pairs)

    def body(hidden_states, clip_lengths, modulation, fc1_weight, fc2_weight, out_grad):
        tok_rows, width = hidden_states.shape
        clip_count = modulation.shape[0]
        full_width = width * cols
        r = lax.axis_index("row")
        c = lax.axis_index("col")
        z, core = c // 2, c % 2

        lens = jnp.concatenate(
            [clip_lengths] + [over_row(clip_lengths, i) for i in range(1, rows)], axis=0
        )

        def segment_of(lengths):
            places = lax.broadcasted_iota(jnp.int32, (tok_rows, 1), 0)
            segment = jnp.zeros((tok_rows, 1), jnp.int32)
            end = 0
            for i in range(clip_count):
                end = end + lengths[i]
                segment = segment + (places >= end).astype(jnp.int32)
            return segment

        segment = segment_of(clip_lengths[0])
        live = (segment < clip_count).astype(F32)
        member = [(segment == i).astype(F32) for i in range(clip_count)]

        def per_token(vectors):
            return sum(member[i] * vectors[i : i + 1].astype(F32) for i in range(clip_count))

        x_here = hidden_states.astype(F32)
        g_here = out_grad.astype(F32)

        fill = -(tok_rows + 2 * clip_count) % 16
        long_rows = tok_rows + 2 * clip_count + fill
        packed = jnp.concatenate(
            [hidden_states, modulation[:, 0], modulation[:, 1], jnp.zeros((fill, width), BF)], axis=0
        )
        chunks = jnp.stack([packed] + [over_z(packed, i) for i in range(1, depth)])

        half = 2 * width
        assert fc1_weight.shape[0] == half
        first_own = lax.dynamic_slice_in_dim(fc1_weight, core * width, width, 0)
        first_other = lax.dynamic_slice_in_dim(fc1_weight, (1 - core) * width, width, 0)
        second_own = lax.dynamic_slice_in_dim(fc2_weight, core * width, width, 1)
        second_other = lax.dynamic_slice_in_dim(fc2_weight, (1 - core) * width, width, 1)

        x_part = chunks[:, :tok_rows].astype(F32)
        mean_part = jnp.mean(x_part, axis=(0, 2))
        spread = x_part - mean_part[None, :, None]
        square_part = jnp.sum(spread * spread, axis=(0, 2))
        theirs = over_core(jnp.stack([mean_part, square_part]))
        centre = 0.5 * (mean_part + theirs[0])
        gap = mean_part - theirs[0]
        square = square_part + theirs[1] + gap * gap * (full_width / 4)
        inverse = lax.rsqrt(square / full_width + epsilon)[:, None]
        centre = centre[:, None]

        def message(j):
            chunk = lax.dynamic_index_in_dim(chunks, z ^ j, 0, keepdims=False)
            shift = per_token(chunk[tok_rows : tok_rows + clip_count])
            scale = per_token(chunk[tok_rows + clip_count : tok_rows + 2 * clip_count])
            x = chunk[:tok_rows].astype(F32)
            modulated = ((x - centre) * inverse * (1.0 + scale) + shift).astype(BF)
            return jnp.concatenate([modulated, chunk[tok_rows:]], axis=0)

        messages = [message(r ^ i) for i in range(rows)]

        counts = jnp.minimum(jnp.sum(lens, axis=1), tok_rows)
        total_live = jnp.sum(counts)
        step = max(16, tok_rows * rows // 32)
        sizes = list(range(tok_rows // 2, tok_rows + 1, step))
        if sizes[-1] != tok_rows:
            sizes.append(tok_rows)
        choice = sum((total_live > rows * size).astype(jnp.int32) for size in sizes[:-1])

        def branch(size):
            total = rows * size

            def run(lens, messages, out_grad, modulation, weights, hidden_states, centre, inverse):
                first_own, first_other, second_own, second_other = weights
                x_here = hidden_states.astype(F32)
                g_here = out_grad.astype(F32)
                gate_here = per_token(modulation[:, 2])
                scale_here = per_token(modulation[:, 1])
                normed = (x_here - centre) * inverse

                index = lax.broadcasted_iota(jnp.int32, (total, 1), 0)
                slot = ((index // size) ^ r) * size + index % size
                counts = jnp.minimum(jnp.sum(lens, axis=1), tok_rows)
                near = jnp.arange(rows, dtype=jnp.int32)
                place_row = near ^ r
                start = jnp.sum(
                    jnp.where(place_row[None, :] < place_row[:, None], counts[None, :], 0), axis=1
                )
                tri = jnp.arange(clip_count)[None, :] <= jnp.arange(clip_count)[:, None]
                ends = start[:, None] + jnp.sum(
                    jnp.where(tri[None], lens[:, None, :], 0), axis=2
                )
                begins = ends - lens

                def slots_of(starts, numbers, height):
                    places = lax.broadcasted_iota(jnp.int32, (rows, height), 1)
                    return jnp.where(places < numbers[:, None], starts[:, None] + places, -1)

                def pick(height):
                    at = slots_of(start, counts, height).reshape(1, rows * height)
                    return slot == at

                wide = pick(long_rows).astype(BF)
                plain = pick(tok_rows).astype(BF)
                place = lax.broadcasted_iota(jnp.int32, (rows, long_rows), 1)

                def clip_rows(offset):
                    low = jnp.full((rows, long_rows), -1, jnp.int32)
                    high = low
                    for i in range(clip_count):
                        here = place == tok_rows + offset * clip_count + i
                        low = jnp.where(here, begins[:, i : i + 1], low)
                        high = jnp.where(here, ends[:, i : i + 1], high)
                    low = low.reshape(1, rows * long_rows)
                    high = high.reshape(1, rows * long_rows)
                    return ((slot >= low) & (slot < high)).astype(BF)

                def share(pieces):
                    return jnp.concatenate(pieces, axis=0)

                rows_in = share([messages[0]] + [over_row(messages[i], i) for i in range(1, rows)])
                mod_own = dot(wide, rows_in).astype(BF)
                mod_other = over_core(mod_own)

                z_grad = (live * gate_here * g_here).astype(BF)
                z_grad, _ = lax.optimization_barrier((z_grad, messages[-1]))
                z_chunks = jnp.stack([z_grad] + [over_z(z_grad, i) for i in range(1, depth)])

                def z_pick(i):
                    return lax.dynamic_index_in_dim(z_chunks, z ^ r ^ i, 0, keepdims=False)

                z_in = share([z_pick(0)] + [over_row(z_pick(i), i) for i in range(1, rows)])
                z_own = dot(plain, z_in).astype(BF)
                z_other = over_core(z_own)

                def scatter_rows(value):
                    parts = value.reshape(rows, size, value.shape[1])
                    came = [over_row(parts[i].astype(BF), i) for i in range(1, rows)]
                    return sum((p.astype(F32) for p in came), parts[0])

                def gather_rows(value):
                    return share([value] + [over_row(value, i) for i in range(1, rows)])

                pre_act = scatter_rows(dot(mod_own, first_own) + dot(mod_other, first_other))
                act_grad = scatter_rows(dot_t(z_own, second_own) + dot_t(z_other, second_other))
                activated, slope = gelu_and_slope(pre_act)
                act_all = gather_rows(activated.astype(BF))
                pre_grad_all = gather_rows((act_grad * slope).astype(BF))

                unpack_start = []
                unpack_count = []
                for i in range(depth):
                    here = place_row == (z ^ i)
                    unpack_start.append(jnp.sum(jnp.where(here, start, 0)))
                    unpack_count.append(jnp.sum(jnp.where(here, counts, 0)))
                out_at = slots_of(jnp.stack(unpack_start), jnp.stack(unpack_count), tok_rows)
                unpack = (slot.reshape(1, total) == out_at.reshape(depth * tok_rows, 1)).astype(BF)

                def to_owner(given, kept):
                    both = kept + over_core(given.astype(BF)).astype(F32)
                    spread = dot(unpack, both.astype(BF)).reshape(depth, tok_rows, width)
                    total_here = spread[0]
                    for i in range(1, depth):
                        total_here = total_here + over_z(spread[i].astype(BF), i).astype(F32)
                    return both, transpose_owner(total_here.astype(BF)).astype(F32)

                _, projected = to_owner(dot(act_all, second_other), dot(act_all, second_own))
                both, mod_in_grad = to_owner(
                    dot_t(pre_grad_all, first_other), dot_t(pre_grad_all, first_own)
                )

                scaled = 1.0 + dot(clip_rows(1), rows_in)
                scaled_normed = dot(wide - clip_rows(0), rows_in)
                sums = jnp.stack(
                    [jnp.sum(both * scaled, axis=1), jnp.sum(both * scaled_normed, axis=1)]
                )
                moved = sums.reshape(2, rows, size)

                def common(value):
                    return jnp.stack(
                        [
                            jnp.sum(
                                jnp.where((place_row == t)[None, :, None], value, 0.0), axis=1
                            )
                            for t in range(rows)
                        ],
                        axis=1,
                    )

                whole = common(moved)
                whole = whole + sum(over_row(whole, i) for i in range(1, rows))
                whole = whole + over_core(whole)
                whole = whole + sum(over_z(whole, i) for i in range(1, depth))
                flat = whole.reshape(2, 1, total)
                own_at = start[0] + lax.broadcasted_iota(jnp.int32, (tok_rows, total), 0)
                hit = own_at == lax.broadcasted_iota(jnp.int32, (tok_rows, total), 1)
                means = jnp.sum(jnp.where(hit[None], flat, 0.0), axis=2) / full_width
                first_mean = means[0][:, None]
                second_mean = means[1][:, None]

                block_out = (live * (x_here + gate_here * projected)).astype(BF)
                norm_grad = mod_in_grad * (1.0 + scale_here)
                input_grad = (
                    live * (g_here + inverse * (norm_grad - first_mean - normed * second_mean))
                ).astype(BF)

                def per_clip(values):
                    return jnp.stack(
                        [jnp.sum(member[i] * values, axis=0) for i in range(clip_count)]
                    )

                modulation_grad = jnp.stack(
                    [
                        per_clip(mod_in_grad),
                        per_clip(mod_in_grad * normed),
                        per_clip(projected * g_here),
                    ],
                    axis=1,
                )
                return block_out, input_grad, modulation_grad

            return run

        return lax.switch(
            choice,
            [branch(size) for size in sizes],
            lens,
            messages,
            out_grad,
            modulation,
            (first_own, first_other, second_own, second_other),
            hidden_states,
            centre,
            inverse,
        )

    return body


def solution(mesh):
    rows, cols = mesh.shape["row"], mesh.shape["col"]
    return jax.shard_map(
        make_body(rows, cols),
        mesh=mesh,
        in_specs=(
            P("row", "col"),
            P("row", None),
            P("row", None, "col"),
            P("row", "col"),
            P("col", "row"),
            P("row", "col"),
        ),
        out_specs=(P("row", "col"), P("row", "col"), P("row", None, "col")),
        check_vma=False,
    )
```

```python
import jax
import jax.numpy as jnp
from jax import lax
from jax.experimental.layout import Layout, with_layout_constraint
from jax.sharding import PartitionSpec as P

epsilon = 1e-06
BF = jnp.bfloat16
F32 = jnp.float32


def gelu_and_slope(value):
    coeff = 0.7978845608028654
    inner = coeff * (value + 0.044715 * value * value * value)
    tangent = jnp.tanh(inner)
    half = 0.5 * (1.0 + tangent)
    slope = half + 0.5 * value * (1.0 - tangent * tangent) * coeff * (
        1.0 + 3.0 * 0.044715 * value * value
    )
    return value * half, slope


def dot(a, b):
    return jnp.dot(a, b, preferred_element_type=F32)


def dot_t(a, b):
    return lax.dot_general(a, b, (((1,), (1,)), ((), ())), preferred_element_type=F32)


def after(value, *events):
    return lax.optimization_barrier((value, *events))[0]


def row_major(value):
    return with_layout_constraint(value, Layout(major_to_minor=(0, 1)))


def flips_of(size):
    return [1 << bit for bit in range(size.bit_length() - 1)]


def reduce_steps(move, sides, orders, events=None):
    sides = [dict(enumerate(side)) for side in sides]
    marks = ()
    for flips in zip(*orders):
        came = []
        for side, flip in zip(sides, flips):
            sent = [j for j in sorted(side) if j & flip]
            sent = jnp.stack([side.pop(j).astype(BF) for j in sent])
            if marks and events:
                sent = after(sent, *events(marks))
            came.append(move(sent, flip))
        if len(came) > 1:
            came = lax.optimization_barrier(tuple(came))
        marks = marks + (tuple(came),)
        for side, got in zip(sides, came):
            for place, j in enumerate(sorted(side)):
                side[j] = side[j].astype(F32) + got[place].astype(F32)
    return [side[0] for side in sides], marks


def gather_steps(move, values, orders, events=None):
    sides = [{0: value} for value in values]
    marks = ()
    for flips in zip(*orders):
        came = []
        for side, flip in zip(sides, flips):
            sent = jnp.stack([side[j] for j in sorted(side)])
            if marks and events:
                sent = after(sent, *events(marks))
            came.append(move(sent, flip))
        if len(came) > 1:
            came = lax.optimization_barrier(tuple(came))
        marks = marks + (tuple(came),)
        for side, got, flip in zip(sides, came, flips):
            for place, j in enumerate(sorted(side)):
                side[j ^ flip] = got[place]
    return [[side[j] for j in range(len(side))] for side in sides], marks


def make_body(rows, cols):
    depth = cols // 2
    assert depth == rows and rows & (rows - 1) == 0
    up = flips_of(rows)
    down = up[::-1]

    def over_row(value, flip):
        return lax.ppermute(value, "row", [(i, i ^ flip) for i in range(rows)])

    def over_z(value, flip):
        return lax.ppermute(value, "col", [(i, i ^ (2 * flip)) for i in range(cols)])

    def over_core(value):
        return lax.ppermute(value, "col", [(i, i ^ 1) for i in range(cols)])

    def scatter_rows(share, tok_rows, events=None):
        half = tok_rows // 2
        parts = share.reshape(rows, tok_rows, share.shape[1])
        sides = [[parts[j, :half] for j in range(rows)], [parts[j, half:] for j in range(rows)]]
        sums, marks = reduce_steps(over_row, sides, [up, down], events)
        return jnp.concatenate(sums, axis=0), marks

    def gather_rows(value, events=None):
        half = value.shape[0] // 2
        sides, marks = gather_steps(over_row, [value[:half], value[half:]], [up, down], events)
        return jnp.concatenate([s[j] for j in range(rows) for s in sides], axis=0), marks

    def gather_z(value):
        sides, _ = gather_steps(over_z, [value], [down])
        return jnp.stack(sides[0])

    def body(hidden_states, clip_lengths, modulation, fc1_weight, fc2_weight, out_grad):
        tok_rows, width = hidden_states.shape
        clip_count = modulation.shape[0]
        full_width = width * cols
        r = lax.axis_index("row")
        c = lax.axis_index("col")
        z, core = c // 2, c % 2

        places = lax.broadcasted_iota(jnp.int32, (tok_rows, 1), 0)
        member, end = [], 0
        for i in range(clip_count):
            begin, end = end, end + clip_lengths[0, i]
            member.append(((places >= begin) & (places < end)).astype(F32))
        live = sum(member)

        def per_token(vectors):
            return sum(member[i] * vectors[i : i + 1].astype(F32) for i in range(clip_count))

        x_here = hidden_states.astype(F32)
        g_here = out_grad.astype(F32)
        scale_here = per_token(modulation[:, 1])
        gate_here = per_token(modulation[:, 2])

        last = tok_rows + 2 * clip_count
        packed = jnp.concatenate(
            [
                hidden_states,
                modulation[:, 0],
                modulation[:, 1],
                jnp.zeros((-last % 16, width), BF),
            ],
            axis=0,
        )
        with jax.named_scope("x_over_z"):
            chunks = jnp.stack([packed] + [over_z(packed, i) for i in range(1, depth)])
        z_grad = (live * gate_here * g_here).astype(BF)

        def own_and_other(weight):
            own = lax.dynamic_slice_in_dim(weight, core * width, width, 1)
            other = lax.dynamic_slice_in_dim(weight, (1 - core) * width, width, 1)
            return row_major(own), row_major(other)

        first_own, first_other = own_and_other(fc1_weight.T)
        second_own, second_other = own_and_other(fc2_weight)
        chunks = after(chunks, first_own, first_other)

        x_part = chunks[:, :tok_rows].astype(F32)
        mean_part = jnp.mean(x_part, axis=(0, 2))
        spread = x_part - mean_part[None, :, None]
        square_part = jnp.sum(spread * spread, axis=(0, 2))
        theirs = over_core(jnp.stack([mean_part, square_part]))
        centre = 0.5 * (mean_part + theirs[0])
        gap = mean_part - theirs[0]
        square = square_part + theirs[1] + gap * gap * (full_width / 4)
        inverse = lax.rsqrt(square / full_width + epsilon)[:, None]
        centre = centre[:, None]
        normed = (x_here - centre) * inverse

        def message(j):
            chunk = lax.dynamic_index_in_dim(chunks, z ^ j, 0, keepdims=False)
            shift = per_token(chunk[tok_rows : tok_rows + clip_count])
            scale = per_token(chunk[tok_rows + clip_count : last])
            x = chunk[:tok_rows].astype(F32)
            return ((x - centre) * inverse * (1.0 + scale) + shift).astype(BF)

        with jax.named_scope("modulated_over_row"):
            arrived = [message(r)] + [over_row(message(r ^ i), i) for i in range(1, rows)]
        arrived[-1] = after(arrived[-1], second_own, second_other)
        mod_own = lax.optimization_barrier(jnp.concatenate(arrived, axis=0))
        mod_other = over_core(mod_own)

        pre_share = dot_t(mod_own, first_own) + dot_t(mod_other, first_other)
        pre_share = row_major(pre_share.astype(BF))
        z_grad = after(z_grad, pre_share)
        with jax.named_scope("z_grad_over_z"):
            z_came = [over_z(z_grad, i) for i in range(1, depth)]
            z_chunks = jnp.stack([z_grad] + z_came)
        with jax.named_scope("pre_act_scatter"):
            pre_act, scatter_marks = scatter_rows(pre_share, tok_rows)
        z_chunks = after(z_chunks, *scatter_marks[0])

        def z_pick(i):
            return lax.dynamic_index_in_dim(z_chunks, r ^ z ^ i, 0, keepdims=False)

        with jax.named_scope("z_grad_over_row"):
            z_arrived = [over_row(z_pick(i), i) for i in range(1, rows)]
        z_own = jnp.concatenate([z_pick(0)] + z_arrived, axis=0)
        z_own = lax.optimization_barrier(z_own)
        z_other = over_core(z_own)

        act_share = dot_t(z_own, second_own) + dot_t(z_other, second_other)
        act_share = row_major(act_share.astype(BF))
        act_share = after(act_share, *scatter_marks[-1])
        activated, slope = gelu_and_slope(pre_act)
        with jax.named_scope("activated_gather"):
            act_all, gather_marks = gather_rows(activated.astype(BF))
        with jax.named_scope("act_grad_scatter"):
            act_grad, act_marks = scatter_rows(act_share, tok_rows, lambda marks: gather_marks[0])
        pre_grad = after((act_grad * slope).astype(BF), *gather_marks[-1])

        def core_sum(given, kept):
            kept = lax.optimization_barrier(kept)
            both = kept + over_core(given.astype(BF)).astype(F32)
            return both.reshape(rows, tok_rows, width)

        def to_rows(both):
            both = both.astype(BF)
            return jnp.stack([both[0]] + [over_row(both[i], i) for i in range(1, rows)])

        def groups_of(parts):
            return [
                lax.dynamic_index_in_dim(parts, r ^ z ^ i, 0, keepdims=False) for i in range(depth)
            ]

        def to_depth(groups, events=None):
            (total,), marks = reduce_steps(over_z, [groups], [up], events)
            return total, marks

        act_all = after(act_all, act_share)
        out_both = core_sum(dot(act_all, second_other), dot(act_all, second_own))
        out_both = out_both.astype(BF)
        with jax.named_scope("projected_home"):
            projected, depth_marks = to_depth(groups_of(to_rows(after(out_both, *act_marks[-1]))))
        with jax.named_scope("pre_grad_gather"):
            pre_grad_all, _ = gather_rows(pre_grad, lambda marks: (out_both,))
        in_both = core_sum(dot(pre_grad_all, first_other), dot(pre_grad_all, first_own))
        with jax.named_scope("in_grad_to_row"):
            in_groups = groups_of(to_rows(in_both))
        first_sum = jnp.zeros((tok_rows,), F32)
        second_sum = jnp.zeros((tok_rows,), F32)
        for i in range(depth):
            share = in_groups[i].astype(F32)
            chunk = chunks[i]
            scaled = 1.0 + per_token(chunk[tok_rows + clip_count : last])
            share = share * scaled
            first_sum = first_sum + jnp.sum(share, axis=1)
            deviation = chunk[:tok_rows].astype(F32) - centre
            second_sum = second_sum + jnp.sum(share * deviation, axis=1)
        sums = jnp.stack([first_sum, second_sum * inverse[:, 0]])
        with jax.named_scope("norm_sums"):
            sums = sums + over_core(sums)
            for flip in up:
                sums = sums + over_z(sums, flip)
        with jax.named_scope("in_grad_over_z"):
            mod_in_grad, _ = to_depth([after(in_groups[0], *depth_marks[0]), *in_groups[1:]], lambda marks: (sums,))
        projected = after(projected, mod_in_grad)
        norm_grad = mod_in_grad * (1.0 + scale_here)
        first_mean = (sums[0] / full_width)[:, None]
        second_mean = (sums[1] / full_width)[:, None]
        input_grad = (
            live * (g_here + inverse * (norm_grad - first_mean - normed * second_mean))
        ).astype(BF)
        block_out = (live * (x_here + gate_here * projected)).astype(BF)

        def per_clip(values):
            return jnp.stack([jnp.sum(member[i] * values, axis=0) for i in range(clip_count)])

        modulation_grad = jnp.stack(
            [per_clip(mod_in_grad), per_clip(mod_in_grad * normed), per_clip(projected * g_here)],
            axis=1,
        )
        return block_out, input_grad, modulation_grad

    return body


def solution(mesh):
    rows, cols = mesh.shape["row"], mesh.shape["col"]
    return jax.shard_map(
        make_body(rows, cols),
        mesh=mesh,
        in_specs=(
            P("row", "col"),
            P("row", None),
            P("row", None, "col"),
            P("row", "col"),
            P("col", "row"),
            P("row", "col"),
        ),
        out_specs=(P("row", "col"), P("row", "col"), P("row", None, "col")),
        check_vma=False,
    )
```

```python
import jax
import jax.numpy as jnp
from jax import lax
from jax.experimental.layout import Layout, with_layout_constraint
from jax.sharding import PartitionSpec as P

epsilon = 1e-06
BF = jnp.bfloat16
F32 = jnp.float32


def gelu_and_slope(value):
    coeff = 0.7978845608028654
    inner = coeff * (value + 0.044715 * value * value * value)
    tangent = jnp.tanh(inner)
    half = 0.5 * (1.0 + tangent)
    slope = half + 0.5 * value * (1.0 - tangent * tangent) * coeff * (
        1.0 + 3.0 * 0.044715 * value * value
    )
    return value * half, slope


def dot(a, b):
    return jnp.dot(a, b, preferred_element_type=F32)


def dot_t(a, b):
    return lax.dot_general(a, b, (((1,), (1,)), ((), ())), preferred_element_type=F32)


def after(value, *events):
    return lax.optimization_barrier((value, *events))[0]


def row_major(value):
    return with_layout_constraint(value, Layout(major_to_minor=(0, 1)))


def flips_of(size):
    return [1 << bit for bit in range(size.bit_length() - 1)]


def reduce_steps(move, sides, orders, events=None):
    sides = [dict(enumerate(side)) for side in sides]
    marks = ()
    for flips in zip(*orders):
        came = []
        for side, flip in zip(sides, flips):
            sent = [j for j in sorted(side) if j & flip]
            sent = jnp.stack([side.pop(j).astype(BF) for j in sent])
            if marks and events:
                sent = after(sent, *events(marks))
            came.append(move(sent, flip))
        if len(came) > 1:
            came = lax.optimization_barrier(tuple(came))
        marks = marks + (tuple(came),)
        for side, got in zip(sides, came):
            for place, j in enumerate(sorted(side)):
                side[j] = side[j].astype(F32) + got[place].astype(F32)
    return [side[0] for side in sides], marks


def gather_steps(move, values, orders, events=None):
    sides = [{0: value} for value in values]
    marks = ()
    for flips in zip(*orders):
        came = []
        for side, flip in zip(sides, flips):
            sent = jnp.stack([side[j] for j in sorted(side)])
            if marks and events:
                sent = after(sent, *events(marks))
            came.append(move(sent, flip))
        if len(came) > 1:
            came = lax.optimization_barrier(tuple(came))
        marks = marks + (tuple(came),)
        for side, got, flip in zip(sides, came, flips):
            for place, j in enumerate(sorted(side)):
                side[j ^ flip] = got[place]
    return [[side[j] for j in range(len(side))] for side in sides], marks


def make_body(rows, cols):
    depth = cols // 2
    assert depth == rows and rows & (rows - 1) == 0
    up = flips_of(rows)
    down = up[::-1]

    def over_row(value, flip):
        return lax.ppermute(value, "row", [(i, i ^ flip) for i in range(rows)])

    def over_z(value, flip):
        return lax.ppermute(value, "col", [(i, i ^ (2 * flip)) for i in range(cols)])

    def over_core(value):
        return lax.ppermute(value, "col", [(i, i ^ 1) for i in range(cols)])

    def scatter_rows(share, tok_rows, events=None):
        half = tok_rows // 2
        parts = share.reshape(rows, tok_rows, share.shape[1])
        sides = [[parts[j, :half] for j in range(rows)], [parts[j, half:] for j in range(rows)]]
        sums, marks = reduce_steps(over_row, sides, [up, down], events)
        return jnp.concatenate(sums, axis=0), marks

    def gather_rows(value, events=None):
        half = value.shape[0] // 2
        sides, marks = gather_steps(over_row, [value[:half], value[half:]], [up, down], events)
        return jnp.concatenate([s[j] for j in range(rows) for s in sides], axis=0), marks

    def gather_z(value):
        sides, _ = gather_steps(over_z, [value], [down])
        return jnp.stack(sides[0])

    def body(hidden_states, clip_lengths, modulation, fc1_weight, fc2_weight, out_grad):
        tok_rows, width = hidden_states.shape
        clip_count = modulation.shape[0]
        full_width = width * cols
        r = lax.axis_index("row")
        c = lax.axis_index("col")
        z, core = c // 2, c % 2

        places = lax.broadcasted_iota(jnp.int32, (tok_rows, 1), 0)
        member, end = [], 0
        for i in range(clip_count):
            begin, end = end, end + clip_lengths[0, i]
            member.append(((places >= begin) & (places < end)).astype(F32))
        live = sum(member)

        def per_token(vectors):
            return sum(member[i] * vectors[i : i + 1].astype(F32) for i in range(clip_count))

        x_here = hidden_states.astype(F32)
        g_here = out_grad.astype(F32)
        scale_here = per_token(modulation[:, 1])
        gate_here = per_token(modulation[:, 2])

        last = tok_rows + 2 * clip_count
        packed = jnp.concatenate(
            [
                hidden_states,
                modulation[:, 0],
                modulation[:, 1],
                jnp.zeros((-last % 16, width), BF),
            ],
            axis=0,
        )
        with jax.named_scope("x_over_z"):
            chunks = jnp.stack([packed] + [over_z(packed, i) for i in range(1, depth)])
        z_grad = (live * gate_here * g_here).astype(BF)

        def own_and_other(weight):
            own = lax.dynamic_slice_in_dim(weight, core * width, width, 1)
            other = lax.dynamic_slice_in_dim(weight, (1 - core) * width, width, 1)
            return row_major(own), row_major(other)

        first_own, first_other = own_and_other(fc1_weight.T)
        second_own, second_other = own_and_other(fc2_weight)
        chunks = after(chunks, first_own, first_other)

        x_part = chunks[:, :tok_rows].astype(F32)
        mean_part = jnp.mean(x_part, axis=(0, 2))
        spread = x_part - mean_part[None, :, None]
        square_part = jnp.sum(spread * spread, axis=(0, 2))
        theirs = over_core(jnp.stack([mean_part, square_part]))
        centre = 0.5 * (mean_part + theirs[0])
        gap = mean_part - theirs[0]
        square = square_part + theirs[1] + gap * gap * (full_width / 4)
        inverse = lax.rsqrt(square / full_width + epsilon)[:, None]
        centre = centre[:, None]
        normed = (x_here - centre) * inverse

        def message(j):
            chunk = lax.dynamic_index_in_dim(chunks, z ^ j, 0, keepdims=False)
            shift = per_token(chunk[tok_rows : tok_rows + clip_count])
            scale = per_token(chunk[tok_rows + clip_count : last])
            x = chunk[:tok_rows].astype(F32)
            return ((x - centre) * inverse * (1.0 + scale) + shift).astype(BF)

        with jax.named_scope("modulated_over_row"):
            arrived = [message(r)] + [over_row(message(r ^ i), i) for i in range(1, rows)]
        arrived[-1] = after(arrived[-1], second_own, second_other)
        mod_own = lax.optimization_barrier(jnp.concatenate(arrived, axis=0))
        mod_other = over_core(mod_own)

        pre_share = dot_t(mod_own, first_own) + dot_t(mod_other, first_other)
        pre_share = row_major(pre_share.astype(BF))
        z_grad = after(z_grad, pre_share)
        with jax.named_scope("z_grad_over_z"):
            z_came = [over_z(z_grad, i) for i in range(1, depth)]
            z_chunks = jnp.stack([z_grad] + z_came)
        with jax.named_scope("pre_act_scatter"):
            pre_act, scatter_marks = scatter_rows(pre_share, tok_rows)
        z_chunks = after(z_chunks, *scatter_marks[0])

        def z_pick(i):
            return lax.dynamic_index_in_dim(z_chunks, r ^ z ^ i, 0, keepdims=False)

        with jax.named_scope("z_grad_over_row"):
            z_arrived = [over_row(z_pick(i), i) for i in range(1, rows)]
        z_own = jnp.concatenate([z_pick(0)] + z_arrived, axis=0)
        z_own = lax.optimization_barrier(z_own)
        z_other = over_core(z_own)

        act_share = dot_t(z_own, second_own) + dot_t(z_other, second_other)
        act_share = row_major(act_share.astype(BF))
        act_share = after(act_share, *scatter_marks[-1])
        activated, slope = gelu_and_slope(pre_act)
        with jax.named_scope("activated_gather"):
            act_all, gather_marks = gather_rows(activated.astype(BF))
        with jax.named_scope("act_grad_scatter"):
            act_grad, act_marks = scatter_rows(act_share, tok_rows, lambda marks: gather_marks[0])
        pre_grad = after((act_grad * slope).astype(BF), *gather_marks[-1])

        def core_sum(given, kept):
            kept = lax.optimization_barrier(kept)
            both = kept + over_core(given.astype(BF)).astype(F32)
            return both.reshape(rows, tok_rows, width)

        def to_rows(both):
            both = both.astype(BF)
            return jnp.stack([both[0]] + [over_row(both[i], i) for i in range(1, rows)])

        def groups_of(parts):
            return [
                lax.dynamic_index_in_dim(parts, r ^ z ^ i, 0, keepdims=False) for i in range(depth)
            ]

        def to_depth(groups, events=None):
            (total,), marks = reduce_steps(over_z, [groups], [up], events)
            return total, marks

        act_all = after(act_all, act_share)
        out_both = core_sum(dot(act_all, second_other), dot(act_all, second_own))
        out_both = out_both.astype(BF)
        with jax.named_scope("projected_home"):
            out_groups = groups_of(to_rows(after(out_both, *act_marks[-1])))
            projected, depth_marks = to_depth(out_groups)
        with jax.named_scope("pre_grad_gather"):
            pre_grad_all, _ = gather_rows(pre_grad, lambda marks: (out_both,))
        in_both = core_sum(dot(pre_grad_all, first_other), dot(after(pre_grad_all, *depth_marks[0]), first_own))
        with jax.named_scope("in_grad_to_row"):
            in_groups = groups_of(to_rows(in_both))
        first_sum = jnp.zeros((tok_rows,), F32)
        second_sum = jnp.zeros((tok_rows,), F32)
        for i in range(depth):
            share = in_groups[i].astype(F32)
            chunk = chunks[i]
            scaled = 1.0 + per_token(chunk[tok_rows + clip_count : last])
            share = share * scaled
            first_sum = first_sum + jnp.sum(share, axis=1)
            deviation = chunk[:tok_rows].astype(F32) - centre
            second_sum = second_sum + jnp.sum(share * deviation, axis=1)
        sums = jnp.stack([first_sum, second_sum * inverse[:, 0]])
        with jax.named_scope("norm_sums"):
            sums = sums + over_core(sums)
        whole = after(sums, *depth_marks[1])
        with jax.named_scope("norm_sums"):
            whole = whole + sum(over_z(whole, i) for i in range(1, depth))
        with jax.named_scope("in_grad_over_z"):
            mod_in_grad, _ = to_depth(
                [after(in_groups[0], *depth_marks[0]), *in_groups[1:]], lambda marks: (whole,)
            )
        projected = after(projected, mod_in_grad)
        norm_grad = mod_in_grad * (1.0 + scale_here)
        first_mean = (whole[0] / full_width)[:, None]
        second_mean = (whole[1] / full_width)[:, None]
        input_grad = (
            live * (g_here + inverse * (norm_grad - first_mean - normed * second_mean))
        ).astype(BF)
        block_out = (live * (x_here + gate_here * projected)).astype(BF)

        def per_clip(values):
            return jnp.stack([jnp.sum(member[i] * values, axis=0) for i in range(clip_count)])

        modulation_grad = jnp.stack(
            [per_clip(mod_in_grad), per_clip(mod_in_grad * normed), per_clip(projected * g_here)],
            axis=1,
        )
        return block_out, input_grad, modulation_grad

    return body


def solution(mesh):
    rows, cols = mesh.shape["row"], mesh.shape["col"]
    return jax.shard_map(
        make_body(rows, cols),
        mesh=mesh,
        in_specs=(
            P("row", "col"),
            P("row", None),
            P("row", None, "col"),
            P("row", "col"),
            P("col", "row"),
            P("row", "col"),
        ),
        out_specs=(P("row", "col"), P("row", "col"), P("row", None, "col")),
        check_vma=False,
    )
```

```python
import jax
import jax.numpy as jnp
from jax import lax
from jax.experimental.layout import Layout, with_layout_constraint
from jax.sharding import PartitionSpec as P

epsilon = 1e-06
BF = jnp.bfloat16
F32 = jnp.float32


def gelu_and_slope(value):
    coeff = 0.7978845608028654
    inner = coeff * (value + 0.044715 * value * value * value)
    tangent = jnp.tanh(inner)
    half = 0.5 * (1.0 + tangent)
    slope = half + 0.5 * value * (1.0 - tangent * tangent) * coeff * (
        1.0 + 3.0 * 0.044715 * value * value
    )
    return value * half, slope


def dot(a, b):
    return jnp.dot(a, b, preferred_element_type=F32)


def dot_t(a, b):
    return lax.dot_general(a, b, (((1,), (1,)), ((), ())), preferred_element_type=F32)


def after(value, *events):
    return lax.optimization_barrier((value, *events))[0]


def row_major(value):
    return with_layout_constraint(value, Layout(major_to_minor=(0, 1)))


def flips_of(size):
    return [1 << bit for bit in range(size.bit_length() - 1)]


def reduce_steps(move, sides, orders, events=None):
    sides = [dict(enumerate(side)) for side in sides]
    marks = ()
    for flips in zip(*orders):
        came = []
        for side, flip in zip(sides, flips):
            sent = [j for j in sorted(side) if j & flip]
            sent = jnp.stack([side.pop(j).astype(BF) for j in sent])
            if marks and events:
                sent = after(sent, *events(marks))
            came.append(move(sent, flip))
        if len(came) > 1:
            came = lax.optimization_barrier(tuple(came))
        marks = marks + (tuple(came),)
        for side, got in zip(sides, came):
            for place, j in enumerate(sorted(side)):
                side[j] = side[j].astype(F32) + got[place].astype(F32)
    return [side[0] for side in sides], marks


def gather_steps(move, values, orders, events=None):
    sides = [{0: value} for value in values]
    marks = ()
    for flips in zip(*orders):
        came = []
        for side, flip in zip(sides, flips):
            sent = jnp.stack([side[j] for j in sorted(side)])
            if marks and events:
                sent = after(sent, *events(marks))
            came.append(move(sent, flip))
        if len(came) > 1:
            came = lax.optimization_barrier(tuple(came))
        marks = marks + (tuple(came),)
        for side, got, flip in zip(sides, came, flips):
            for place, j in enumerate(sorted(side)):
                side[j ^ flip] = got[place]
    return [[side[j] for j in range(len(side))] for side in sides], marks


def make_body(rows, cols):
    depth = cols // 2
    assert depth == rows and rows & (rows - 1) == 0
    up = flips_of(rows)
    down = up[::-1]

    def over_row(value, flip):
        return lax.ppermute(value, "row", [(i, i ^ flip) for i in range(rows)])

    def over_z(value, flip):
        return lax.ppermute(value, "col", [(i, i ^ (2 * flip)) for i in range(cols)])

    def over_core(value):
        return lax.ppermute(value, "col", [(i, i ^ 1) for i in range(cols)])

    def scatter_rows(share, tok_rows, events=None):
        half = tok_rows // 2
        parts = share.reshape(rows, tok_rows, share.shape[1])
        sides = [[parts[j, :half] for j in range(rows)], [parts[j, half:] for j in range(rows)]]
        sums, marks = reduce_steps(over_row, sides, [up, down], events)
        return jnp.concatenate(sums, axis=0), marks

    def gather_rows(value, events=None):
        half = value.shape[0] // 2
        sides, marks = gather_steps(over_row, [value[:half], value[half:]], [up, down], events)
        return jnp.concatenate([s[j] for j in range(rows) for s in sides], axis=0), marks

    def gather_z(value):
        sides, _ = gather_steps(over_z, [value], [down])
        return jnp.stack(sides[0])

    def body(hidden_states, clip_lengths, modulation, fc1_weight, fc2_weight, out_grad):
        tok_rows, width = hidden_states.shape
        clip_count = modulation.shape[0]
        full_width = width * cols
        r = lax.axis_index("row")
        c = lax.axis_index("col")
        z, core = c // 2, c % 2

        places = lax.broadcasted_iota(jnp.int32, (tok_rows, 1), 0)
        member, end = [], 0
        for i in range(clip_count):
            begin, end = end, end + clip_lengths[0, i]
            member.append(((places >= begin) & (places < end)).astype(F32))
        live = sum(member)

        def per_token(vectors):
            return sum(member[i] * vectors[i : i + 1].astype(F32) for i in range(clip_count))

        x_here = hidden_states.astype(F32)
        g_here = out_grad.astype(F32)
        scale_here = per_token(modulation[:, 1])
        gate_here = per_token(modulation[:, 2])

        last = tok_rows + 2 * clip_count
        packed = jnp.concatenate(
            [
                hidden_states,
                modulation[:, 0],
                modulation[:, 1],
                jnp.zeros((-last % 16, width), BF),
            ],
            axis=0,
        )
        with jax.named_scope("x_over_z"):
            chunks = jnp.stack([packed] + [over_z(packed, i) for i in range(1, depth)])
        z_grad = (live * gate_here * g_here).astype(BF)

        def own_and_other(weight):
            own = lax.dynamic_slice_in_dim(weight, core * width, width, 1)
            other = lax.dynamic_slice_in_dim(weight, (1 - core) * width, width, 1)
            return row_major(own), row_major(other)

        first_own, first_other = own_and_other(fc1_weight.T)
        second_own, second_other = own_and_other(fc2_weight)
        chunks = after(chunks, first_own, first_other)

        x_part = chunks[:, :tok_rows].astype(F32)
        mean_part = jnp.mean(x_part, axis=(0, 2))
        spread = x_part - mean_part[None, :, None]
        square_part = jnp.sum(spread * spread, axis=(0, 2))
        theirs = over_core(jnp.stack([mean_part, square_part]))
        centre = 0.5 * (mean_part + theirs[0])
        gap = mean_part - theirs[0]
        square = square_part + theirs[1] + gap * gap * (full_width / 4)
        inverse = lax.rsqrt(square / full_width + epsilon)[:, None]
        centre = centre[:, None]
        normed = (x_here - centre) * inverse

        def message(j):
            chunk = lax.dynamic_index_in_dim(chunks, z ^ j, 0, keepdims=False)
            shift = per_token(chunk[tok_rows : tok_rows + clip_count])
            scale = per_token(chunk[tok_rows + clip_count : last])
            x = chunk[:tok_rows].astype(F32)
            return ((x - centre) * inverse * (1.0 + scale) + shift).astype(BF)

        with jax.named_scope("modulated_over_row"):
            arrived = [message(r)] + [over_row(message(r ^ i), i) for i in range(1, rows)]
        arrived[-1] = after(arrived[-1], second_own, second_other)
        mod_own = lax.optimization_barrier(jnp.concatenate(arrived, axis=0))
        mod_other = over_core(mod_own)

        pre_share = dot_t(mod_own, first_own) + dot_t(mod_other, first_other)
        pre_share = row_major(pre_share.astype(BF))
        z_grad = after(z_grad, pre_share)
        with jax.named_scope("z_grad_over_z"):
            z_came = [over_z(z_grad, i) for i in range(1, depth)]
            z_chunks = jnp.stack([z_grad] + z_came)
        with jax.named_scope("pre_act_scatter"):
            pre_act, scatter_marks = scatter_rows(pre_share, tok_rows)
        z_chunks = after(z_chunks, *scatter_marks[0])

        def z_pick(i):
            return lax.dynamic_index_in_dim(z_chunks, r ^ z ^ i, 0, keepdims=False)

        with jax.named_scope("z_grad_over_row"):
            z_arrived = [over_row(z_pick(i), i) for i in range(1, rows)]
        z_own = jnp.concatenate([z_pick(0)] + z_arrived, axis=0)
        z_own = lax.optimization_barrier(z_own)
        z_other = over_core(z_own)

        act_share = dot_t(z_own, second_own) + dot_t(z_other, second_other)
        act_share = row_major(act_share.astype(BF))
        act_share = after(act_share, *scatter_marks[-1])
        activated, slope = gelu_and_slope(pre_act)
        with jax.named_scope("activated_gather"):
            act_all, gather_marks = gather_rows(activated.astype(BF))
        with jax.named_scope("act_grad_scatter"):
            act_grad, act_marks = scatter_rows(act_share, tok_rows, lambda marks: gather_marks[0])
        pre_grad = after((act_grad * slope).astype(BF), *gather_marks[-1])

        def core_sum(given, kept):
            kept = lax.optimization_barrier(kept)
            both = kept + over_core(given.astype(BF)).astype(F32)
            return both.reshape(rows, tok_rows, width)

        def to_rows(both):
            both = both.astype(BF)
            return jnp.stack([both[0]] + [over_row(both[i], i) for i in range(1, rows)])

        def groups_of(parts):
            return [
                lax.dynamic_index_in_dim(parts, r ^ z ^ i, 0, keepdims=False) for i in range(depth)
            ]

        def to_depth(groups, events=None):
            (total,), marks = reduce_steps(over_z, [groups], [up], events)
            return total, marks

        act_all = after(act_all, act_share)
        out_both = core_sum(dot(act_all, second_other), dot(act_all, second_own))
        out_both = out_both.astype(BF)
        with jax.named_scope("projected_home"):
            out_groups = groups_of(to_rows(after(out_both, *act_marks[-1])))
            projected, depth_marks = to_depth(out_groups)
        with jax.named_scope("pre_grad_gather"):
            pre_grad_all, _ = gather_rows(pre_grad, lambda marks: (out_both,))
        in_both = core_sum(dot(pre_grad_all, first_other), dot(after(pre_grad_all, *depth_marks[0]), first_own))
        with jax.named_scope("in_grad_to_row"):
            in_groups = groups_of(to_rows(in_both))
        first_sum = jnp.zeros((tok_rows,), F32)
        second_sum = jnp.zeros((tok_rows,), F32)
        for i in range(depth):
            share = in_groups[i].astype(F32)
            chunk = chunks[i]
            scaled = 1.0 + per_token(chunk[tok_rows + clip_count : last])
            share = share * scaled
            first_sum = first_sum + jnp.sum(share, axis=1)
            deviation = chunk[:tok_rows].astype(F32) - centre
            second_sum = second_sum + jnp.sum(share * deviation, axis=1)
        sums = jnp.stack([first_sum, second_sum * inverse[:, 0]])
        with jax.named_scope("norm_sums"):
            sums = sums + over_core(sums)
        whole = after(sums, *depth_marks[1])
        with jax.named_scope("norm_sums"):
            whole = whole + sum(over_z(whole, i) for i in range(1, depth))
        with jax.named_scope("in_grad_over_z"):
            mod_in_grad, _ = to_depth(
                [in_groups[0], *in_groups[1:]], lambda marks: (whole,)
            )
        projected = after(projected, mod_in_grad)
        norm_grad = mod_in_grad * (1.0 + scale_here)
        first_mean = (whole[0] / full_width)[:, None]
        second_mean = (whole[1] / full_width)[:, None]
        input_grad = (
            live * (g_here + inverse * (norm_grad - first_mean - normed * second_mean))
        ).astype(BF)
        block_out = (live * (x_here + gate_here * projected)).astype(BF)

        def per_clip(values):
            return jnp.stack([jnp.sum(member[i] * values, axis=0) for i in range(clip_count)])

        modulation_grad = jnp.stack(
            [per_clip(mod_in_grad), per_clip(mod_in_grad * normed), per_clip(projected * g_here)],
            axis=1,
        )
        return block_out, input_grad, modulation_grad

    return body


def solution(mesh):
    rows, cols = mesh.shape["row"], mesh.shape["col"]
    return jax.shard_map(
        make_body(rows, cols),
        mesh=mesh,
        in_specs=(
            P("row", "col"),
            P("row", None),
            P("row", None, "col"),
            P("row", "col"),
            P("col", "row"),
            P("row", "col"),
        ),
        out_specs=(P("row", "col"), P("row", "col"), P("row", None, "col")),
        check_vma=False,
    )
```

```python
import jax
import jax.numpy as jnp
from jax import lax
from jax.experimental.layout import Layout, with_layout_constraint
from jax.sharding import PartitionSpec as P

epsilon = 1e-06
BF = jnp.bfloat16
F32 = jnp.float32


def gelu_and_slope(value):
    coeff = 0.7978845608028654
    inner = coeff * (value + 0.044715 * value * value * value)
    tangent = jnp.tanh(inner)
    half = 0.5 * (1.0 + tangent)
    slope = half + 0.5 * value * (1.0 - tangent * tangent) * coeff * (
        1.0 + 3.0 * 0.044715 * value * value
    )
    return value * half, slope


def dot(a, b):
    return jnp.dot(a, b, preferred_element_type=F32)


def dot_t(a, b):
    return lax.dot_general(a, b, (((1,), (1,)), ((), ())), preferred_element_type=F32)


def after(value, *events):
    return lax.optimization_barrier((value, *events))[0]


def row_major(value):
    return with_layout_constraint(value, Layout(major_to_minor=(0, 1)))


def flips_of(size):
    return [1 << bit for bit in range(size.bit_length() - 1)]


def reduce_steps(move, sides, orders, events=None):
    sides = [dict(enumerate(side)) for side in sides]
    marks = ()
    for flips in zip(*orders):
        came = []
        for side, flip in zip(sides, flips):
            sent = [j for j in sorted(side) if j & flip]
            sent = jnp.stack([side.pop(j).astype(BF) for j in sent])
            if marks and events:
                sent = after(sent, *events(marks))
            came.append(move(sent, flip))
        if len(came) > 1:
            came = lax.optimization_barrier(tuple(came))
        marks = marks + (tuple(came),)
        for side, got in zip(sides, came):
            for place, j in enumerate(sorted(side)):
                side[j] = side[j].astype(F32) + got[place].astype(F32)
    return [side[0] for side in sides], marks


def gather_steps(move, values, orders, events=None):
    sides = [{0: value} for value in values]
    marks = ()
    for flips in zip(*orders):
        came = []
        for side, flip in zip(sides, flips):
            sent = jnp.stack([side[j] for j in sorted(side)])
            if marks and events:
                sent = after(sent, *events(marks))
            came.append(move(sent, flip))
        if len(came) > 1:
            came = lax.optimization_barrier(tuple(came))
        marks = marks + (tuple(came),)
        for side, got, flip in zip(sides, came, flips):
            for place, j in enumerate(sorted(side)):
                side[j ^ flip] = got[place]
    return [[side[j] for j in range(len(side))] for side in sides], marks


def make_body(rows, cols):
    depth = cols // 2
    assert depth == rows and rows & (rows - 1) == 0
    up = flips_of(rows)
    down = up[::-1]

    def over_row(value, flip):
        return lax.ppermute(value, "row", [(i, i ^ flip) for i in range(rows)])

    def over_z(value, flip):
        return lax.ppermute(value, "col", [(i, i ^ (2 * flip)) for i in range(cols)])

    def over_core(value):
        return lax.ppermute(value, "col", [(i, i ^ 1) for i in range(cols)])

    def scatter_rows(share, tok_rows, events=None):
        half = tok_rows // 2
        parts = share.reshape(rows, tok_rows, share.shape[1])
        sides = [[parts[j, :half] for j in range(rows)], [parts[j, half:] for j in range(rows)]]
        sums, marks = reduce_steps(over_row, sides, [up, down], events)
        return jnp.concatenate(sums, axis=0), marks

    def gather_rows(value, events=None):
        half = value.shape[0] // 2
        sides, marks = gather_steps(over_row, [value[:half], value[half:]], [up, down], events)
        return jnp.concatenate([s[j] for j in range(rows) for s in sides], axis=0), marks

    def gather_z(value):
        sides, _ = gather_steps(over_z, [value], [down])
        return jnp.stack(sides[0])

    def body(hidden_states, clip_lengths, modulation, fc1_weight, fc2_weight, out_grad):
        tok_rows, width = hidden_states.shape
        clip_count = modulation.shape[0]
        full_width = width * cols
        r = lax.axis_index("row")
        c = lax.axis_index("col")
        z, core = c // 2, c % 2

        places = lax.broadcasted_iota(jnp.int32, (tok_rows, 1), 0)
        member, end = [], 0
        for i in range(clip_count):
            begin, end = end, end + clip_lengths[0, i]
            member.append(((places >= begin) & (places < end)).astype(F32))
        live = sum(member)

        def per_token(vectors):
            return sum(member[i] * vectors[i : i + 1].astype(F32) for i in range(clip_count))

        x_here = hidden_states.astype(F32)
        g_here = out_grad.astype(F32)
        scale_here = per_token(modulation[:, 1])
        gate_here = per_token(modulation[:, 2])

        last = tok_rows + 2 * clip_count
        packed = jnp.concatenate(
            [
                hidden_states,
                modulation[:, 0],
                modulation[:, 1],
                jnp.zeros((-last % 16, width), BF),
            ],
            axis=0,
        )
        with jax.named_scope("x_over_z"):
            chunks = jnp.stack([packed] + [over_z(packed, i) for i in range(1, depth)])
        z_grad = (live * gate_here * g_here).astype(BF)

        def own_and_other(weight):
            own = lax.dynamic_slice_in_dim(weight, core * width, width, 1)
            other = lax.dynamic_slice_in_dim(weight, (1 - core) * width, width, 1)
            return row_major(own), row_major(other)

        first_own, first_other = own_and_other(fc1_weight.T)
        second_own, second_other = own_and_other(fc2_weight)
        chunks = after(chunks, first_own, first_other)

        x_part = chunks[:, :tok_rows].astype(F32)
        mean_part = jnp.mean(x_part, axis=(0, 2))
        spread = x_part - mean_part[None, :, None]
        square_part = jnp.sum(spread * spread, axis=(0, 2))
        theirs = over_core(jnp.stack([mean_part, square_part]))
        centre = 0.5 * (mean_part + theirs[0])
        gap = mean_part - theirs[0]
        square = square_part + theirs[1] + gap * gap * (full_width / 4)
        inverse = lax.rsqrt(square / full_width + epsilon)[:, None]
        centre = centre[:, None]
        normed = (x_here - centre) * inverse

        def message(j):
            chunk = lax.dynamic_index_in_dim(chunks, z ^ j, 0, keepdims=False)
            shift = per_token(chunk[tok_rows : tok_rows + clip_count])
            scale = per_token(chunk[tok_rows + clip_count : last])
            x = chunk[:tok_rows].astype(F32)
            return ((x - centre) * inverse * (1.0 + scale) + shift).astype(BF)

        with jax.named_scope("modulated_over_row"):
            arrived = [message(r)] + [over_row(message(r ^ i), i) for i in range(1, rows)]
        arrived[-1] = after(arrived[-1], second_own, second_other)
        mod_own = lax.optimization_barrier(jnp.concatenate(arrived, axis=0))
        mod_other = over_core(mod_own)

        pre_share = dot_t(mod_own, first_own) + dot_t(mod_other, first_other)
        pre_share = row_major(pre_share.astype(BF))
        z_grad = after(z_grad, pre_share)
        with jax.named_scope("z_grad_over_z"):
            z_came = [over_z(z_grad, i) for i in range(1, depth)]
            z_chunks = jnp.stack([z_grad] + z_came)
        with jax.named_scope("pre_act_scatter"):
            pre_act, scatter_marks = scatter_rows(pre_share, tok_rows)
        z_chunks = after(z_chunks, *scatter_marks[0])

        def z_pick(i):
            return lax.dynamic_index_in_dim(z_chunks, r ^ z ^ i, 0, keepdims=False)

        with jax.named_scope("z_grad_over_row"):
            z_arrived = [over_row(z_pick(i), i) for i in range(1, rows)]
        z_own = jnp.concatenate([z_pick(0)] + z_arrived, axis=0)
        z_own = lax.optimization_barrier(z_own)
        z_other = over_core(z_own)

        act_share = dot_t(z_own, second_own) + dot_t(z_other, second_other)
        act_share = row_major(act_share.astype(BF))
        act_share = after(act_share, *scatter_marks[-1])
        activated, slope = gelu_and_slope(pre_act)
        with jax.named_scope("activated_gather"):
            act_all, gather_marks = gather_rows(activated.astype(BF))
        with jax.named_scope("act_grad_scatter"):
            act_grad, act_marks = scatter_rows(act_share, tok_rows, lambda marks: gather_marks[0])
        pre_grad = after((act_grad * slope).astype(BF), *gather_marks[-1])

        def core_sum(given, kept):
            kept = lax.optimization_barrier(kept)
            both = kept + over_core(given.astype(BF)).astype(F32)
            return both.reshape(rows, tok_rows, width)

        def to_rows(both):
            both = both.astype(BF)
            return jnp.stack([both[0]] + [over_row(both[i], i) for i in range(1, rows)])

        def groups_of(parts):
            return [
                lax.dynamic_index_in_dim(parts, r ^ z ^ i, 0, keepdims=False) for i in range(depth)
            ]

        def to_depth(groups, events=None):
            (total,), marks = reduce_steps(over_z, [groups], [up], events)
            return total, marks

        act_all = after(act_all, act_share)
        out_both = core_sum(dot(act_all, second_other), dot(act_all, second_own))
        out_both = out_both.astype(BF)
        with jax.named_scope("projected_home"):
            out_groups = groups_of(to_rows(after(out_both, *act_marks[-1])))
            projected, depth_marks = to_depth(out_groups)
        with jax.named_scope("pre_grad_gather"):
            pre_grad_all, _ = gather_rows(pre_grad, lambda marks: (out_both,))
        in_both = core_sum(dot(pre_grad_all, first_other), dot(after(pre_grad_all, *depth_marks[0]), first_own))
        with jax.named_scope("in_grad_to_row"):
            in_groups = groups_of(to_rows(in_both))
        first_sum = jnp.zeros((tok_rows,), F32)
        second_sum = jnp.zeros((tok_rows,), F32)
        for i in range(depth):
            share = in_groups[i].astype(F32)
            chunk = chunks[i]
            scaled = 1.0 + per_token(chunk[tok_rows + clip_count : last])
            share = share * scaled
            first_sum = first_sum + jnp.sum(share, axis=1)
            deviation = chunk[:tok_rows].astype(F32) - centre
            second_sum = second_sum + jnp.sum(share * deviation, axis=1)
        sums = jnp.stack([first_sum, second_sum * inverse[:, 0]])
        with jax.named_scope("norm_sums"):
            sums = sums + over_core(sums)
        whole = after(sums, *depth_marks[0])
        with jax.named_scope("norm_sums"):
            whole = whole + sum(over_z(whole, i) for i in range(1, depth))
        with jax.named_scope("in_grad_over_z"):
            mod_in_grad, _ = to_depth(
                [in_groups[0], *in_groups[1:]], lambda marks: (whole,)
            )
        projected = after(projected, mod_in_grad)
        norm_grad = mod_in_grad * (1.0 + scale_here)
        first_mean = (whole[0] / full_width)[:, None]
        second_mean = (whole[1] / full_width)[:, None]
        input_grad = (
            live * (g_here + inverse * (norm_grad - first_mean - normed * second_mean))
        ).astype(BF)
        block_out = (live * (x_here + gate_here * projected)).astype(BF)

        def per_clip(values):
            return jnp.stack([jnp.sum(member[i] * values, axis=0) for i in range(clip_count)])

        modulation_grad = jnp.stack(
            [per_clip(mod_in_grad), per_clip(mod_in_grad * normed), per_clip(projected * g_here)],
            axis=1,
        )
        return block_out, input_grad, modulation_grad

    return body


def solution(mesh):
    rows, cols = mesh.shape["row"], mesh.shape["col"]
    return jax.shard_map(
        make_body(rows, cols),
        mesh=mesh,
        in_specs=(
            P("row", "col"),
            P("row", None),
            P("row", None, "col"),
            P("row", "col"),
            P("col", "row"),
            P("row", "col"),
        ),
        out_specs=(P("row", "col"), P("row", "col"), P("row", None, "col")),
        check_vma=False,
    )
```
